32 devices in a mesh: layer: 8 (over z, x), batch: 4 (over y, core).
Axes of the slice: x: 2, y: 2, z: 4, core: 2. Of those that a mesh axis runs over, the one named last changes fastest.
Arguments:
- first_state: float32 [4, 32, 32, 256], P('batch'), may hold values from -6 to 6
- guess_points: float32 [8, 4, 32, 32, 256], P('layer', 'batch'), may hold values from -6 to 6
- weights: bfloat16 [32, 3, 3, 256, 256], P('layer'), may hold values from -0.5 to 0.5
Outputs:
- states: float32 [32, 4, 32, 32, 256], P('layer', 'batch')
- norms: float32 [8], P('layer')
The draws below stay inside these ranges and needn't reach their ends.
All inputs are finite; a program needn't handle non-finite values.
Results may differ from the reference program's by a relative error of at most 0.0038.
Values sent between devices are 32-bit elements; how exact they have to be, the bound alone decides.
A program may use at most 128 MiB of HBM per device.

```python
import jax
import jax.numpy as jnp
from jax import lax

CH = 256
IMG = 32
BLOCK = 4
BLOCKS = 8
GROUPS = 2
LAYERS = 32
BATCH = 4


def levels(stream_key, extent, pieces, least, top_value):
    loudness, own = 1.0, jax.random.fold_in(stream_key, 6)
    for position, parts in pieces:
        heights = jnp.exp(jax.random.uniform(jax.random.fold_in(own, position), (parts,), jnp.float32, least / len(pieces), top_value / len(pieces)))
        loudness = loudness * jnp.repeat(heights, extent[position] // parts).reshape([-1 if axis == position else 1 for axis in range(len(extent))])
    return loudness


def scatter_about(stream_key, shape, width, bound, pieces=(), kind=jnp.bfloat16):
    result = jax.random.normal(stream_key, shape, jnp.float32) * width
    if len(pieces) > 0:
        result = levels(stream_key, shape, pieces, -0.22, 0.18) * result
    return jnp.clip(result, min=-bound, max=bound).astype(kind)


def setup_inputs(seed: int = 0) -> dict:
    key_list = jax.random.split(jax.random.key(seed), 4)
    return {
        "first_state": scatter_about(key_list[0], (BATCH, IMG, IMG, CH), 1.0, 6.0, ((0, 4),), jnp.float32),
        "guess_points": scatter_about(key_list[1], (BLOCKS, BATCH, IMG, IMG, CH), 1.0, 6.0, ((0, 8), (1, 4)), jnp.float32),
        "weights": scatter_about(key_list[2], (LAYERS, 3, 3, CH, CH), (9 * CH // 16) ** -0.5, 0.5, ((0, 8),)),
    }


def propagate(state, weight, factor):
    mixed = lax.conv_general_dilated(state.astype(jnp.bfloat16), weight, (1, 1), 'SAME', dimension_numbers=('NHWC', 'HWIO', 'NHWC'), preferred_element_type=jnp.float32)
    return state + factor * jax.nn.relu(mixed)

def shifted(first_state, stacked):
    return jnp.concatenate([first_state[None], stacked[:-1]], axis=0)

def reference(first_state, guess_points, weights):
    vstep = jax.vmap(propagate, in_axes=(0, 0, None))
    step_size = 2.0 / LAYERS
    blocked = weights.reshape(BLOCKS, BLOCK, 3, 3, CH, CH)

    def block_sweep(state):
        for slot in range(BLOCK):
            state = vstep(state, blocked[:, slot], step_size)
        return state
    relaxed = block_sweep(shifted(first_state, guess_points))
    entry_state = shifted(first_state, relaxed)
    swept = block_sweep(entry_state)
    residual = swept - relaxed
    norms = jnp.sqrt(lax.optimization_barrier(jnp.sum(residual * residual, axis=(1, 2, 3, 4))) / (BATCH * IMG * IMG * CH) + 1e-06)
    fine_rhs = swept - vstep(entry_state, blocked[:, 0], 4.0 * step_size)
    group_weights = blocked[:, 0].reshape(GROUPS, BLOCK, 3, 3, CH, CH)
    group_rhs_fine = fine_rhs.reshape(GROUPS, BLOCK, BATCH, IMG, IMG, CH)

    def group_sweep(state, length):
        results = []
        for slot in range(length):
            state = vstep(state, group_weights[:, slot], 4.0 * step_size) + group_rhs_fine[:, slot]
            results.append(state)
        return results
    group_entry = shifted(first_state, relaxed[BLOCK - 1::BLOCK])
    group_ends = group_sweep(group_entry, BLOCK)[-1]
    previous_ends = shifted(first_state, group_ends)
    group_rhs = group_sweep(previous_ends, BLOCK)[-1] - vstep(previous_ends, group_weights[:, 0], 16.0 * step_size)
    coarse_state = first_state
    coarse_list = []
    for group in range(GROUPS):
        coarse_state = propagate(coarse_state, group_weights[group, 0], 16.0 * step_size) + group_rhs[group]
        coarse_list.append(coarse_state)
    coarse_states = jnp.stack(coarse_list)
    corrected = group_sweep(shifted(first_state, coarse_states), BLOCK - 1)
    corrected.append(coarse_states)
    coarse_final = jnp.stack(corrected, axis=1).reshape(BLOCKS, BATCH, IMG, IMG, CH)
    moving = shifted(first_state, coarse_final)
    results = []
    for slot in range(BLOCK - 1):
        moving = vstep(moving, blocked[:, slot], step_size)
        results.append(moving)
    results.append(coarse_final)
    states = jnp.stack(results, axis=1).reshape(LAYERS, BATCH, IMG, IMG, CH)
    return (states, norms)
```

```python
import functools

import jax
import jax.numpy as jnp
from jax import lax
from jax.experimental import pallas as pl
from jax.experimental.pallas import tpu as pltpu
from jax.sharding import PartitionSpec as P

BLOCK = 4


def passed_along(block, axis, distance):
    devices = range(lax.axis_size(axis))
    route = [(i - distance, i) for i in devices if i - distance in devices]
    return lax.ppermute(block, axis, route)


def propagate(state, weight, factor):
    mixed = lax.conv_general_dilated(
        state.astype(jnp.bfloat16),
        weight,
        (1, 1),
        "SAME",
        dimension_numbers=("NHWC", "HWIO", "NHWC"),
        preferred_element_type=jnp.float32,
    )
    return state + factor * jax.nn.relu(mixed)


def per_device(first_state, guess_points, weights):
    blocks_here = lax.axis_size("layer")
    step_size = 2.0 / (BLOCK * blocks_here)
    layer_index = lax.axis_index("layer")
    position = layer_index % 4
    is_first = layer_index == 0
    zeros_state = jnp.zeros_like(first_state)

    def block_sweep(state):
        for slot in range(BLOCK):
            state = propagate(state, weights[slot], step_size)
        return state

    from_left = passed_along(guess_points[0], "layer", 1)
    relaxed = block_sweep(jnp.where(is_first, first_state, from_left))
    from_left = passed_along(relaxed, "layer", 1)
    entry_state = jnp.where(is_first, first_state, from_left)
    swept = block_sweep(entry_state)
    residual = swept - relaxed
    square_sum = lax.psum(jnp.sum(residual * residual), "batch")
    entries = residual.size * lax.axis_size("batch")
    norms = jnp.reshape(jnp.sqrt(square_sum / entries + 1e-06), (1,))
    coarse_weight = weights[0]
    fine_rhs = swept - propagate(entry_state, coarse_weight, 4.0 * step_size)

    def coarse_apply(state):
        return propagate(state, coarse_weight, 4.0 * step_size) + fine_rhs

    def coarse_chain(carry_out, length):
        moving = zeros_state
        taken = zeros_state
        for turn_index in range(length):
            outgoing = jnp.where(position == 3, carry_out, moving)
            received = passed_along(outgoing, "layer", 1)
            incoming = jnp.where(is_first, first_state, received)
            moving = lax.cond(
                position == turn_index,
                lambda fresh, kept: coarse_apply(fresh),
                lambda fresh, kept: kept,
                incoming,
                moving,
            )
            taken = jnp.where(position == turn_index, incoming, taken)
        return (moving, taken)

    group_ends, unused_taken = coarse_chain(relaxed, BLOCK)
    swept_ends, previous_ends = coarse_chain(group_ends, BLOCK)
    predicted = lax.cond(
        position == 0,
        lambda state: propagate(state, coarse_weight, 16.0 * step_size),
        lambda state: jnp.zeros_like(state),
        previous_ends,
    )

    def coarse_delta(received_state):
        earlier = jnp.where(is_first, first_state, received_state)
        return (earlier, propagate(earlier, coarse_weight, 16.0 * step_size) - predicted)

    def branch_of(turn_index):
        kind = jnp.where(position == 0, 0, jnp.where(position == 3, 2, 1))
        return jnp.where(layer_index == turn_index, kind, 3)

    def relay_single(turn_index, carried):
        sending, own_value = carried
        got = passed_along(sending, "layer", 1)

        def head_step(got_in, sent, kept):
            earlier, delta = coarse_delta(got_in)
            return (delta, kept)

        def middle_step(got_in, sent, kept):
            return (got_in, kept)

        def tail_step(got_in, sent, kept):
            value = got_in + swept_ends
            return (value, value)

        def keep_step(got_in, sent, kept):
            return (sent, kept)

        return lax.switch(
            branch_of(turn_index),
            [head_step, middle_step, tail_step, keep_step],
            got,
            sending,
            own_value,
        )

    sending, coarse_own = lax.fori_loop(0, blocks_here, relay_single, (zeros_state, zeros_state))
    corrected, unused_entry = coarse_chain(coarse_own, BLOCK - 1)
    coarse_final = jnp.where(position == 3, coarse_own, corrected)
    from_left = passed_along(coarse_final, "layer", 1)
    moving = jnp.where(is_first, first_state, from_left)
    results = []
    for slot in range(BLOCK - 1):
        moving = propagate(moving, weights[slot], step_size)
        results.append(moving)
    results.append(coarse_final)
    return (jnp.stack(results), norms)


PASS_ROWS = 8
CHAIN_ROWS = 4


def cycle_kernel(
    layers_axis,
    batch_axis,
    first_ref,
    guess_ref,
    weights_ref,
    out_ref,
    norm_ref,
    guess_in,
    entry_in,
    coarse_in,
    work,
    relaxed_ref,
    rhs_ref,
    taps_a,
    taps_b,
    partial_ref,
    guess_send,
    guess_recv,
    entry_send,
    entry_recv,
    coarse_send,
    coarse_recv,
    norm_send,
    norm_recv,
):
    rows, width, channels = first_ref.shape
    step_size = 2.0 / (BLOCK * layers_axis)
    me = lax.axis_index("layer")
    my_batch = lax.axis_index("batch")
    last = layers_axis - 1
    passes = rows // PASS_ROWS
    pieces = rows // CHAIN_ROWS

    def strip(index, count):
        return pl.ds(pl.multiple_of(index * count, count), count)

    def to_right(source, target, send, recv):
        return pltpu.make_async_remote_copy(
            src_ref=source,
            dst_ref=target,
            send_sem=send,
            recv_sem=recv,
            device_id={"layer": me + 1},
            device_id_type=pl.DeviceIdType.MESH,
        )

    def guess_copy(index):
        at = strip(index, PASS_ROWS)
        return to_right(guess_ref.at[at], guess_in.at[at], guess_send.at[index], guess_recv.at[index])

    def entry_copy(index):
        at = strip(index, PASS_ROWS)
        return to_right(relaxed_ref.at[at], entry_in.at[at], entry_send.at[index], entry_recv.at[index])

    def coarse_copy(index):
        at = strip(index, CHAIN_ROWS)
        return to_right(out_ref.at[3, at], coarse_in.at[at], coarse_send.at[index], coarse_recv.at[index])

    def norm_copy(offset):
        return pltpu.make_async_remote_copy(
            src_ref=partial_ref.at[my_batch],
            dst_ref=partial_ref.at[my_batch],
            send_sem=norm_send.at[offset],
            recv_sem=norm_recv.at[offset],
            device_id={"batch": lax.rem(my_batch + offset, batch_axis)},
            device_id_type=pl.DeviceIdType.MESH,
        )

    barrier = pltpu.get_barrier_semaphore()

    @pl.when(me > 0)
    def _():
        pl.semaphore_signal(barrier, inc=1, device_id={"layer": me - 1}, device_id_type=pl.DeviceIdType.MESH)

    @pl.when(me < last)
    def _():
        pl.semaphore_signal(barrier, inc=1, device_id={"layer": me + 1}, device_id_type=pl.DeviceIdType.MESH)

    for offset in range(1, batch_axis):
        pl.semaphore_signal(
            barrier,
            inc=1,
            device_id={"batch": lax.rem(my_batch + offset, batch_axis)},
            device_id_type=pl.DeviceIdType.MESH,
        )
    others = batch_axis - 1 + jnp.where(me > 0, 1, 0) + jnp.where(me < last, 1, 0)
    pl.semaphore_wait(barrier, others)

    @pl.when(me < last)
    def _():
        for index in range(passes):
            guess_copy(index).start()

    @pl.when(me == 0)
    def _():
        guess_in[...] = first_ref[...]
        entry_in[...] = first_ref[...]

    for taps in (taps_a, taps_b):
        edge = jnp.zeros((width, 3 * channels), taps.dtype)
        taps[pl.ds(0, width), :] = edge
        taps[pl.ds((rows + 1) * width, width), :] = edge

    def put_taps(taps, index, count, block):
        flat = block.reshape(count * width, channels)
        column = lax.rem(lax.broadcasted_iota(jnp.int32, flat.shape, 0), width)
        before = jnp.where(column == 0, 0.0, pltpu.roll(flat, 1, 0))
        after = jnp.where(column == width - 1, 0.0, pltpu.roll(flat, count * width - 1, 0))
        at = pl.ds(pl.multiple_of((index * count + 1) * width, width), count * width)
        taps[at, pl.ds(0, channels)] = before.astype(taps.dtype)
        taps[at, pl.ds(channels, channels)] = flat.astype(taps.dtype)
        taps[at, pl.ds(2 * channels, channels)] = after.astype(taps.dtype)

    def mixed(taps, slot, index, count):
        total = None
        for down in range(3):
            at = pl.ds(pl.multiple_of((index * count + down) * width, width), count * width)
            part = jnp.dot(taps[at, :], weights_ref[slot, down], preferred_element_type=jnp.float32)
            total = part if total is None else total + part
        return jnp.maximum(total, 0.0).reshape(count, width, channels)

    def one_pass(taps, slot, count, emit, carry=0, arrive=None):
        if arrive is not None:
            arrive(0)

        def body(index, carry):
            if arrive is not None:

                @pl.when(index + 1 < rows // count)
                def _():
                    arrive(index + 1)

            return emit(index, strip(index, count), mixed(taps, slot, index, count), carry)

        return lax.fori_loop(0, rows // count, body, carry)

    def guess_arrives(index):
        @pl.when(me > 0)
        def _():
            guess_copy(index).wait_recv()

        put_taps(taps_a, index, PASS_ROWS, guess_in[strip(index, PASS_ROWS)])

    def relax_step(source, target, taps_next):
        def emit(index, at, active, carry):
            block = source[at] + step_size * active
            target[at] = block
            if taps_next is not None:
                put_taps(taps_next, index, PASS_ROWS, block)
            else:

                @pl.when(me < last)
                def _():
                    entry_copy(index).start()

            return carry

        return emit

    one_pass(taps_a, 0, PASS_ROWS, relax_step(guess_in, work, taps_b), arrive=guess_arrives)
    one_pass(taps_b, 1, PASS_ROWS, relax_step(work, work, taps_a))
    one_pass(taps_a, 2, PASS_ROWS, relax_step(work, work, taps_b))
    one_pass(taps_b, 3, PASS_ROWS, relax_step(work, relaxed_ref, None))

    def entry_arrives(index):
        @pl.when(me > 0)
        def _():
            entry_copy(index).wait_recv()

        put_taps(taps_a, index, PASS_ROWS, entry_in[strip(index, PASS_ROWS)])

    def sweep_first(index, at, active, carry):
        block = entry_in[at]
        rhs_ref[at] = block + 4.0 * step_size * active
        block = block + step_size * active
        out_ref[0, at] = block
        put_taps(taps_b, index, PASS_ROWS, block)
        return carry

    def sweep_middle(slot, taps_next):
        def emit(index, at, active, carry):
            block = out_ref[slot - 1, at] + step_size * active
            out_ref[slot, at] = block
            put_taps(taps_next, index, PASS_ROWS, block)
            return carry

        return emit

    def sweep_last(index, at, active, squares):
        block = out_ref[2, at] + step_size * active
        out_ref[3, at] = block
        rhs_ref[at] = block - rhs_ref[at]

        @pl.when(jnp.logical_and(me == 1, me < last))
        def _():
            for piece in range(PASS_ROWS // CHAIN_ROWS):
                coarse_copy(index * (PASS_ROWS // CHAIN_ROWS) + piece).start()

        gap = (block - relaxed_ref[at]).reshape(-1, 8, channels)
        return squares + jnp.sum(gap * gap, axis=0)

    one_pass(taps_a, 0, PASS_ROWS, sweep_first, arrive=entry_arrives)
    one_pass(taps_b, 1, PASS_ROWS, sweep_middle(1, taps_a))
    one_pass(taps_a, 2, PASS_ROWS, sweep_middle(2, taps_b))
    squares = one_pass(taps_b, 3, PASS_ROWS, sweep_last, jnp.zeros((8, channels), jnp.float32))
    partial_ref[my_batch] = squares
    for offset in range(1, batch_axis):
        norm_copy(offset).start()

    def coarse_arrives(index):
        coarse_copy(index).wait_recv()
        put_taps(taps_a, index, CHAIN_ROWS, coarse_in[strip(index, CHAIN_ROWS)])

    def chain_emit(index, at, active, carry):
        block = coarse_in[at]
        out_ref[3, at] = block + 4.0 * step_size * active + rhs_ref[at]

        @pl.when(me < last)
        def _():
            coarse_copy(index).start()

        block = block + step_size * active
        out_ref[0, at] = block
        put_taps(taps_b, index, CHAIN_ROWS, block)
        return carry

    def final_emit(index, at, active, carry):
        out_ref[2, at] = out_ref[1, at] + step_size * active
        return carry

    @pl.when(me >= 2)
    def _():
        one_pass(taps_a, 0, CHAIN_ROWS, chain_emit, arrive=coarse_arrives)
        one_pass(taps_b, 1, PASS_ROWS, sweep_middle(1, taps_a))
        one_pass(taps_a, 2, PASS_ROWS, final_emit)

    for offset in range(1, batch_axis):
        norm_copy(offset).wait()
    gathered = partial_ref[0]
    for index in range(1, batch_axis):
        gathered = gathered + partial_ref[index]
    entries = rows * width * channels * batch_axis
    norm_ref[...] = jnp.broadcast_to(jnp.sqrt(jnp.sum(gathered, keepdims=True) / entries + 1e-06), norm_ref.shape)

    @pl.when(me < last)
    def _():
        for index in range(passes):
            guess_copy(index).wait_send()
            entry_copy(index).wait_send()

    @pl.when(jnp.logical_and(me >= 1, me < last))
    def _():
        for index in range(pieces):
            coarse_copy(index).wait_send()


def per_device_streamed(first_state, guess_points, weights):
    layers_axis = lax.axis_size("layer")
    batch_axis = lax.axis_size("batch")
    _, rows, width, channels = first_state.shape
    state = (rows, width, channels)
    taps = ((rows + 2) * width, 3 * channels)
    passes, pieces = rows // PASS_ROWS, rows // CHAIN_ROWS
    in_vmem = pl.BlockSpec(memory_space=pltpu.VMEM)
    states, norms = pl.pallas_call(
        functools.partial(cycle_kernel, layers_axis, batch_axis),
        out_shape=(
            jax.ShapeDtypeStruct((BLOCK,) + state, jnp.float32),
            jax.ShapeDtypeStruct((8, 128), jnp.float32),
        ),
        in_specs=[in_vmem] * 3,
        out_specs=(in_vmem, in_vmem),
        scratch_shapes=[pltpu.VMEM(state, jnp.float32)] * 6
        + [pltpu.VMEM(taps, jnp.bfloat16)] * 2
        + [pltpu.VMEM((batch_axis, 8, channels), jnp.float32)]
        + [pltpu.SemaphoreType.DMA((passes,))] * 4
        + [pltpu.SemaphoreType.DMA((pieces,))] * 2
        + [pltpu.SemaphoreType.DMA((batch_axis,))] * 2,
        compiler_params=pltpu.CompilerParams(
            collective_id=0, has_side_effects=True, vmem_limit_bytes=48 * 1024 * 1024
        ),
    )(first_state[0], guess_points[0, 0], weights.reshape(BLOCK, 3, 3 * channels, channels))
    return (states[:, None], norms[0, :1])


def solution(mesh):
    placed = (
        P("batch", None, None, None),
        P("layer", "batch", None, None, None),
        P("layer", None, None, None, None),
    )
    return jax.shard_map(
        per_device if mesh.shape["layer"] // BLOCK > 2 else per_device_streamed,
        mesh=mesh,
        in_specs=placed,
        out_specs=(P("layer", "batch", None, None, None), P("layer")),
        check_vma=False,
    )
```

```python
import functools

import jax
import jax.numpy as jnp
from jax import lax
from jax.experimental import pallas as pl
from jax.experimental.pallas import tpu as pltpu
from jax.sharding import PartitionSpec as P

BLOCK = 4


def passed_along(block, axis, distance):
    devices = range(lax.axis_size(axis))
    route = [(i - distance, i) for i in devices if i - distance in devices]
    return lax.ppermute(block, axis, route)


def propagate(state, weight, factor):
    mixed = lax.conv_general_dilated(
        state.astype(jnp.bfloat16),
        weight,
        (1, 1),
        "SAME",
        dimension_numbers=("NHWC", "HWIO", "NHWC"),
        preferred_element_type=jnp.float32,
    )
    return state + factor * jax.nn.relu(mixed)


def per_device(first_state, guess_points, weights):
    blocks_here = lax.axis_size("layer")
    step_size = 2.0 / (BLOCK * blocks_here)
    layer_index = lax.axis_index("layer")
    position = layer_index % 4
    is_first = layer_index == 0
    zeros_state = jnp.zeros_like(first_state)

    def block_sweep(state):
        for slot in range(BLOCK):
            state = propagate(state, weights[slot], step_size)
        return state

    from_left = passed_along(guess_points[0], "layer", 1)
    relaxed = block_sweep(jnp.where(is_first, first_state, from_left))
    from_left = passed_along(relaxed, "layer", 1)
    entry_state = jnp.where(is_first, first_state, from_left)
    swept = block_sweep(entry_state)
    residual = swept - relaxed
    square_sum = lax.psum(jnp.sum(residual * residual), "batch")
    entries = residual.size * lax.axis_size("batch")
    norms = jnp.reshape(jnp.sqrt(square_sum / entries + 1e-06), (1,))
    coarse_weight = weights[0]
    fine_rhs = swept - propagate(entry_state, coarse_weight, 4.0 * step_size)

    def coarse_apply(state):
        return propagate(state, coarse_weight, 4.0 * step_size) + fine_rhs

    def coarse_chain(carry_out, length):
        moving = zeros_state
        taken = zeros_state
        for turn_index in range(length):
            outgoing = jnp.where(position == 3, carry_out, moving)
            received = passed_along(outgoing, "layer", 1)
            incoming = jnp.where(is_first, first_state, received)
            moving = lax.cond(
                position == turn_index,
                lambda fresh, kept: coarse_apply(fresh),
                lambda fresh, kept: kept,
                incoming,
                moving,
            )
            taken = jnp.where(position == turn_index, incoming, taken)
        return (moving, taken)

    group_ends, unused_taken = coarse_chain(relaxed, BLOCK)
    swept_ends, previous_ends = coarse_chain(group_ends, BLOCK)
    predicted = lax.cond(
        position == 0,
        lambda state: propagate(state, coarse_weight, 16.0 * step_size),
        lambda state: jnp.zeros_like(state),
        previous_ends,
    )

    def coarse_delta(received_state):
        earlier = jnp.where(is_first, first_state, received_state)
        return (earlier, propagate(earlier, coarse_weight, 16.0 * step_size) - predicted)

    def branch_of(turn_index):
        kind = jnp.where(position == 0, 0, jnp.where(position == 3, 2, 1))
        return jnp.where(layer_index == turn_index, kind, 3)

    def relay_single(turn_index, carried):
        sending, own_value = carried
        got = passed_along(sending, "layer", 1)

        def head_step(got_in, sent, kept):
            earlier, delta = coarse_delta(got_in)
            return (delta, kept)

        def middle_step(got_in, sent, kept):
            return (got_in, kept)

        def tail_step(got_in, sent, kept):
            value = got_in + swept_ends
            return (value, value)

        def keep_step(got_in, sent, kept):
            return (sent, kept)

        return lax.switch(
            branch_of(turn_index),
            [head_step, middle_step, tail_step, keep_step],
            got,
            sending,
            own_value,
        )

    sending, coarse_own = lax.fori_loop(0, blocks_here, relay_single, (zeros_state, zeros_state))
    corrected, unused_entry = coarse_chain(coarse_own, BLOCK - 1)
    coarse_final = jnp.where(position == 3, coarse_own, corrected)
    from_left = passed_along(coarse_final, "layer", 1)
    moving = jnp.where(is_first, first_state, from_left)
    results = []
    for slot in range(BLOCK - 1):
        moving = propagate(moving, weights[slot], step_size)
        results.append(moving)
    results.append(coarse_final)
    return (jnp.stack(results), norms)


PASS_ROWS = 4
CHAIN_ROWS = 2


def cycle_kernel(
    layers_axis,
    batch_axis,
    first_ref,
    guess_ref,
    weights_hbm,
    out_ref,
    norm_ref,
    guess_in,
    entry_in,
    coarse_in,
    work,
    relaxed_ref,
    rhs_ref,
    taps_0,
    taps_1,
    taps_2,
    taps_3,
    squares_ref,
    weights_ref,
    load_sem,
    partial_ref,
    guess_send,
    guess_recv,
    entry_send,
    entry_recv,
    coarse_send,
    coarse_recv,
    norm_send,
    norm_recv,
):
    rows, width, channels = first_ref.shape
    step_size = 2.0 / (BLOCK * layers_axis)
    me = lax.axis_index("layer")
    my_batch = lax.axis_index("batch")
    last = layers_axis - 1
    passes = rows // PASS_ROWS
    pieces = rows // CHAIN_ROWS

    def strip(index, count):
        return pl.ds(pl.multiple_of(index * count, count), count)

    def to_right(source, target, send, recv):
        return pltpu.make_async_remote_copy(
            src_ref=source,
            dst_ref=target,
            send_sem=send,
            recv_sem=recv,
            device_id={"layer": me + 1},
            device_id_type=pl.DeviceIdType.MESH,
        )

    def guess_copy(index):
        at = strip(index, PASS_ROWS)
        return to_right(guess_ref.at[at], guess_in.at[at], guess_send.at[index], guess_recv.at[index])

    def entry_copy(index):
        at = strip(index, PASS_ROWS)
        return to_right(relaxed_ref.at[at], entry_in.at[at], entry_send.at[index], entry_recv.at[index])

    def coarse_copy(index):
        at = strip(index, CHAIN_ROWS)
        return to_right(out_ref.at[3, at], coarse_in.at[at], coarse_send.at[index], coarse_recv.at[index])

    def norm_copy(offset):
        return pltpu.make_async_remote_copy(
            src_ref=partial_ref.at[my_batch],
            dst_ref=partial_ref.at[my_batch],
            send_sem=norm_send.at[offset],
            recv_sem=norm_recv.at[offset],
            device_id={"batch": lax.rem(my_batch + offset, batch_axis)},
            device_id_type=pl.DeviceIdType.MESH,
        )

    load_weights = pltpu.make_async_copy(weights_hbm, weights_ref, load_sem)
    load_weights.start()
    barrier = pltpu.get_barrier_semaphore()

    @pl.when(me > 0)
    def _():
        pl.semaphore_signal(barrier, inc=1, device_id={"layer": me - 1}, device_id_type=pl.DeviceIdType.MESH)

    @pl.when(me < last)
    def _():
        pl.semaphore_signal(barrier, inc=1, device_id={"layer": me + 1}, device_id_type=pl.DeviceIdType.MESH)

    for offset in range(1, batch_axis):
        pl.semaphore_signal(
            barrier,
            inc=1,
            device_id={"batch": lax.rem(my_batch + offset, batch_axis)},
            device_id_type=pl.DeviceIdType.MESH,
        )
    others = batch_axis - 1 + jnp.where(me > 0, 1, 0) + jnp.where(me < last, 1, 0)
    pl.semaphore_wait(barrier, others)

    @pl.when(me < last)
    def _():
        for index in range(passes):
            guess_copy(index).start()

    @pl.when(me == 0)
    def _():
        pltpu.sync_copy(first_ref, guess_in)
        entry_in[...] = guess_in[...]

    for taps in (taps_0, taps_1, taps_2, taps_3):
        edge = jnp.zeros((width, 3 * channels), taps.dtype)
        taps[pl.ds(0, width), :] = edge
        taps[pl.ds((rows + 1) * width, width), :] = edge

    def put_taps(taps, index, count, block):
        flat = block.reshape(count * width, channels)
        column = lax.rem(lax.broadcasted_iota(jnp.int32, flat.shape, 0), width)
        before = jnp.where(column == 0, 0.0, pltpu.roll(flat, 1, 0))
        after = jnp.where(column == width - 1, 0.0, pltpu.roll(flat, count * width - 1, 0))
        at = pl.ds(pl.multiple_of((index * count + 1) * width, width), count * width)
        taps[at, pl.ds(0, channels)] = before.astype(taps.dtype)
        taps[at, pl.ds(channels, channels)] = flat.astype(taps.dtype)
        taps[at, pl.ds(2 * channels, channels)] = after.astype(taps.dtype)

    def mixed(taps, slot, index, count):
        total = None
        for down in range(3):
            at = pl.ds(pl.multiple_of((index * count + down) * width, width), count * width)
            part = jnp.dot(taps[at, :], weights_ref[slot, down], preferred_element_type=jnp.float32)
            total = part if total is None else total + part
        return jnp.maximum(total, 0.0).reshape(count, width, channels)

    def wave(count, arrive, steps):
        chunks = rows // count

        def body(turn, carry):
            @pl.when(turn < chunks)
            def _():
                arrive(turn)

            for behind, (taps, slot, emit) in enumerate(steps):
                index = turn - 1 - behind

                @pl.when(jnp.logical_and(index >= 0, index < chunks))
                def _(index=index, taps=taps, slot=slot, emit=emit):
                    emit(index, strip(index, count), mixed(taps, slot, index, count))

            return carry

        lax.fori_loop(0, chunks + len(steps), body, 0)

    load_weights.wait()

    def guess_arrives(index):
        @pl.when(me > 0)
        def _():
            guess_copy(index).wait_recv()

        put_taps(taps_0, index, PASS_ROWS, guess_in[strip(index, PASS_ROWS)])

    def relax_step(source, taps_next):
        def emit(index, at, active):
            block = source[at] + step_size * active
            work[at] = block
            put_taps(taps_next, index, PASS_ROWS, block)

        return emit

    def relax_last(index, at, active):
        relaxed_ref[at] = work[at] + step_size * active

        @pl.when(me < last)
        def _():
            entry_copy(index).start()

    wave(
        PASS_ROWS,
        guess_arrives,
        (
            (taps_0, 0, relax_step(guess_in, taps_1)),
            (taps_1, 1, relax_step(work, taps_2)),
            (taps_2, 2, relax_step(work, taps_3)),
            (taps_3, 3, relax_last),
        ),
    )

    def entry_arrives(index):
        @pl.when(me > 0)
        def _():
            entry_copy(index).wait_recv()

        put_taps(taps_0, index, PASS_ROWS, entry_in[strip(index, PASS_ROWS)])

    def sweep_first(index, at, active):
        block = entry_in[at]
        rhs_ref[at] = block + 4.0 * step_size * active
        block = block + step_size * active
        out_ref[0, at] = block
        put_taps(taps_1, index, PASS_ROWS, block)

    def sweep_middle(slot, count, taps_next):
        def emit(index, at, active):
            block = out_ref[slot - 1, at] + step_size * active
            out_ref[slot, at] = block
            if taps_next is not None:
                put_taps(taps_next, index, count, block)

        return emit

    def sweep_last(index, at, active):
        block = out_ref[2, at] + step_size * active
        out_ref[3, at] = block
        rhs_ref[at] = block - rhs_ref[at]

        @pl.when(jnp.logical_and(me == 1, me < last))
        def _():
            for piece in range(PASS_ROWS // CHAIN_ROWS):
                coarse_copy(index * (PASS_ROWS // CHAIN_ROWS) + piece).start()

        gap = (block - relaxed_ref[at]).reshape(-1, 8, channels)
        squares_ref[...] += jnp.sum(gap * gap, axis=0)

    squares_ref[...] = jnp.zeros_like(squares_ref)
    wave(
        PASS_ROWS,
        entry_arrives,
        (
            (taps_0, 0, sweep_first),
            (taps_1, 1, sweep_middle(1, PASS_ROWS, taps_2)),
            (taps_2, 2, sweep_middle(2, PASS_ROWS, taps_3)),
            (taps_3, 3, sweep_last),
        ),
    )
    partial_ref[my_batch] = squares_ref[...]
    for offset in range(1, batch_axis):
        norm_copy(offset).start()

    def coarse_arrives(index):
        coarse_copy(index).wait_recv()
        put_taps(taps_0, index, CHAIN_ROWS, coarse_in[strip(index, CHAIN_ROWS)])

    def chain_step(index, at, active):
        block = coarse_in[at]
        out_ref[3, at] = block + 4.0 * step_size * active + rhs_ref[at]

        @pl.when(me < last)
        def _():
            coarse_copy(index).start()

        block = block + step_size * active
        out_ref[0, at] = block
        put_taps(taps_1, index, CHAIN_ROWS, block)

    def run(taps, slot, count, emit):
        def body(index, carry):
            emit(index, strip(index, count), mixed(taps, slot, index, count))
            return carry

        return body

    chain_body = run(taps_0, 0, CHAIN_ROWS, chain_step)
    second_body = run(taps_1, 1, CHAIN_ROWS, sweep_middle(1, CHAIN_ROWS, taps_2))
    third_body = run(taps_2, 2, CHAIN_ROWS, sweep_middle(2, CHAIN_ROWS, None))

    @pl.when(me >= 2)
    def _():
        def body(turn, carry):
            coarse_arrives(turn)

            @pl.when(turn >= 1)
            def _():
                chain_body(turn - 1, 0)

            @pl.when(turn == pieces - 1)
            def _():
                chain_body(turn, 0)

            @pl.when(jnp.logical_and(me == last, turn >= 2))
            def _():
                second_body(turn - 2, 0)

            @pl.when(jnp.logical_and(me == last, turn >= 3))
            def _():
                third_body(turn - 3, 0)

            return carry

        lax.fori_loop(0, pieces, body, 0)

        @pl.when(me == last)
        def _():
            lax.fori_loop(pieces - 2, pieces, second_body, 0)
            lax.fori_loop(pieces - 3, pieces, third_body, 0)

        @pl.when(me < last)
        def _():
            lax.fori_loop(0, passes, run(taps_1, 1, PASS_ROWS, sweep_middle(1, PASS_ROWS, taps_2)), 0)
            lax.fori_loop(0, passes, run(taps_2, 2, PASS_ROWS, sweep_middle(2, PASS_ROWS, None)), 0)

    for offset in range(1, batch_axis):
        norm_copy(offset).wait()
    gathered = partial_ref[0]
    for index in range(1, batch_axis):
        gathered = gathered + partial_ref[index]
    entries = rows * width * channels * batch_axis
    norm_ref[...] = jnp.broadcast_to(jnp.sqrt(jnp.sum(gathered, keepdims=True) / entries + 1e-06), norm_ref.shape)

    @pl.when(me < last)
    def _():
        for index in range(passes):
            guess_copy(index).wait_send()
            entry_copy(index).wait_send()

    @pl.when(jnp.logical_and(me >= 1, me < last))
    def _():
        for index in range(pieces):
            coarse_copy(index).wait_send()


def per_device_streamed(first_state, guess_points, weights):
    layers_axis = lax.axis_size("layer")
    batch_axis = lax.axis_size("batch")
    _, rows, width, channels = first_state.shape
    state = (rows, width, channels)
    taps = ((rows + 2) * width, 3 * channels)
    passes, pieces = rows // PASS_ROWS, rows // CHAIN_ROWS
    in_vmem = pl.BlockSpec(memory_space=pltpu.VMEM)
    states, norms = pl.pallas_call(
        functools.partial(cycle_kernel, layers_axis, batch_axis),
        out_shape=(
            pltpu.VMEM((BLOCK,) + state, jnp.float32),
            jax.ShapeDtypeStruct((8, 128), jnp.float32),
        ),
        in_specs=[pl.BlockSpec(memory_space=pltpu.HBM)] * 3,
        out_specs=(in_vmem, in_vmem),
        scratch_shapes=[pltpu.VMEM(state, jnp.float32)] * 6
        + [pltpu.VMEM(taps, jnp.bfloat16)] * 4
        + [pltpu.VMEM((8, channels), jnp.float32)]
        + [pltpu.VMEM((BLOCK, 3, 3 * channels, channels), jnp.bfloat16), pltpu.SemaphoreType.DMA]
        + [pltpu.VMEM((batch_axis, 8, channels), jnp.float32)]
        + [pltpu.SemaphoreType.DMA((passes,))] * 4
        + [pltpu.SemaphoreType.DMA((pieces,))] * 2
        + [pltpu.SemaphoreType.DMA((batch_axis,))] * 2,
        compiler_params=pltpu.CompilerParams(
            collective_id=0, has_side_effects=True, vmem_limit_bytes=40 * 1024 * 1024
        ),
    )(*(pltpu.with_memory_space_constraint(x, pltpu.HBM) for x in (first_state[0], guess_points[0, 0], weights.reshape(BLOCK, 3, 3 * channels, channels))))
    return (states[:, None], norms[0, :1])


def solution(mesh):
    placed = (
        P("batch", None, None, None),
        P("layer", "batch", None, None, None),
        P("layer", None, None, None, None),
    )
    return jax.shard_map(
        per_device if mesh.shape["layer"] // BLOCK > 2 else per_device_streamed,
        mesh=mesh,
        in_specs=placed,
        out_specs=(P("layer", "batch", None, None, None), P("layer")),
        check_vma=False,
    )
```

```python
import functools

import jax
import jax.numpy as jnp
from jax import lax
from jax.experimental import pallas as pl
from jax.experimental.pallas import tpu as pltpu
from jax.sharding import PartitionSpec as P

BLOCK = 4


def passed_along(block, axis, distance):
    devices = range(lax.axis_size(axis))
    route = [(i - distance, i) for i in devices if i - distance in devices]
    return lax.ppermute(block, axis, route)


def propagate(state, weight, factor):
    mixed = lax.conv_general_dilated(
        state.astype(jnp.bfloat16),
        weight,
        (1, 1),
        "SAME",
        dimension_numbers=("NHWC", "HWIO", "NHWC"),
        preferred_element_type=jnp.float32,
    )
    return state + factor * jax.nn.relu(mixed)


def per_device(first_state, guess_points, weights):
    blocks_here = lax.axis_size("layer")
    step_size = 2.0 / (BLOCK * blocks_here)
    layer_index = lax.axis_index("layer")
    position = layer_index % 4
    is_first = layer_index == 0
    zeros_state = jnp.zeros_like(first_state)

    def block_sweep(state):
        for slot in range(BLOCK):
            state = propagate(state, weights[slot], step_size)
        return state

    from_left = passed_along(guess_points[0], "layer", 1)
    relaxed = block_sweep(jnp.where(is_first, first_state, from_left))
    from_left = passed_along(relaxed, "layer", 1)
    entry_state = jnp.where(is_first, first_state, from_left)
    swept = block_sweep(entry_state)
    residual = swept - relaxed
    square_sum = lax.psum(jnp.sum(residual * residual), "batch")
    entries = residual.size * lax.axis_size("batch")
    norms = jnp.reshape(jnp.sqrt(square_sum / entries + 1e-06), (1,))
    coarse_weight = weights[0]
    fine_rhs = swept - propagate(entry_state, coarse_weight, 4.0 * step_size)

    def coarse_apply(state):
        return propagate(state, coarse_weight, 4.0 * step_size) + fine_rhs

    def coarse_chain(carry_out, length):
        moving = zeros_state
        taken = zeros_state
        for turn_index in range(length):
            outgoing = jnp.where(position == 3, carry_out, moving)
            received = passed_along(outgoing, "layer", 1)
            incoming = jnp.where(is_first, first_state, received)
            moving = lax.cond(
                position == turn_index,
                lambda fresh, kept: coarse_apply(fresh),
                lambda fresh, kept: kept,
                incoming,
                moving,
            )
            taken = jnp.where(position == turn_index, incoming, taken)
        return (moving, taken)

    group_ends, unused_taken = coarse_chain(relaxed, BLOCK)
    swept_ends, previous_ends = coarse_chain(group_ends, BLOCK)
    predicted = lax.cond(
        position == 0,
        lambda state: propagate(state, coarse_weight, 16.0 * step_size),
        lambda state: jnp.zeros_like(state),
        previous_ends,
    )

    def coarse_delta(received_state):
        earlier = jnp.where(is_first, first_state, received_state)
        return (earlier, propagate(earlier, coarse_weight, 16.0 * step_size) - predicted)

    def branch_of(turn_index):
        kind = jnp.where(position == 0, 0, jnp.where(position == 3, 2, 1))
        return jnp.where(layer_index == turn_index, kind, 3)

    def relay_single(turn_index, carried):
        sending, own_value = carried
        got = passed_along(sending, "layer", 1)

        def head_step(got_in, sent, kept):
            earlier, delta = coarse_delta(got_in)
            return (delta, kept)

        def middle_step(got_in, sent, kept):
            return (got_in, kept)

        def tail_step(got_in, sent, kept):
            value = got_in + swept_ends
            return (value, value)

        def keep_step(got_in, sent, kept):
            return (sent, kept)

        return lax.switch(
            branch_of(turn_index),
            [head_step, middle_step, tail_step, keep_step],
            got,
            sending,
            own_value,
        )

    sending, coarse_own = lax.fori_loop(0, blocks_here, relay_single, (zeros_state, zeros_state))
    corrected, unused_entry = coarse_chain(coarse_own, BLOCK - 1)
    coarse_final = jnp.where(position == 3, coarse_own, corrected)
    from_left = passed_along(coarse_final, "layer", 1)
    moving = jnp.where(is_first, first_state, from_left)
    results = []
    for slot in range(BLOCK - 1):
        moving = propagate(moving, weights[slot], step_size)
        results.append(moving)
    results.append(coarse_final)
    return (jnp.stack(results), norms)


PASS_ROWS = 4
CHAIN_ROWS = 2


def cycle_kernel(
    layers_axis,
    batch_axis,
    first_ref,
    guess_ref,
    weights_hbm,
    out_ref,
    norm_ref,
    guess_in,
    entry_in,
    coarse_in,
    work,
    relaxed_ref,
    rhs_ref,
    taps_0,
    taps_1,
    taps_2,
    taps_3,
    squares_ref,
    weights_ref,
    load_sem,
    partial_ref,
    guess_send,
    guess_recv,
    entry_send,
    entry_recv,
    coarse_send,
    coarse_recv,
    norm_send,
    norm_recv,
):
    rows, width, channels = first_ref.shape
    step_size = 2.0 / (BLOCK * layers_axis)
    me = lax.axis_index("layer")
    my_batch = lax.axis_index("batch")
    last = layers_axis - 1
    passes = rows // PASS_ROWS
    pieces = rows // CHAIN_ROWS

    def strip(index, count):
        return pl.ds(pl.multiple_of(index * count, count), count)

    def to_right(source, target, send, recv):
        return pltpu.make_async_remote_copy(
            src_ref=source,
            dst_ref=target,
            send_sem=send,
            recv_sem=recv,
            device_id={"layer": me + 1},
            device_id_type=pl.DeviceIdType.MESH,
        )

    def guess_copy(index):
        at = strip(index, PASS_ROWS)
        return to_right(guess_ref.at[at], guess_in.at[at], guess_send.at[index], guess_recv.at[index])

    def entry_copy(index):
        at = strip(index, PASS_ROWS)
        return to_right(relaxed_ref.at[at], entry_in.at[at], entry_send.at[index], entry_recv.at[index])

    def coarse_copy(index):
        at = strip(index, CHAIN_ROWS)
        return to_right(out_ref.at[3, at], coarse_in.at[at], coarse_send.at[index], coarse_recv.at[index])

    def norm_copy(offset):
        return pltpu.make_async_remote_copy(
            src_ref=partial_ref.at[my_batch],
            dst_ref=partial_ref.at[my_batch],
            send_sem=norm_send.at[offset],
            recv_sem=norm_recv.at[offset],
            device_id={"batch": lax.rem(my_batch + offset, batch_axis)},
            device_id_type=pl.DeviceIdType.MESH,
        )

    load_weights = pltpu.make_async_copy(weights_hbm, weights_ref, load_sem)
    load_weights.start()
    barrier = pltpu.get_barrier_semaphore()

    @pl.when(me > 0)
    def _():
        pl.semaphore_signal(barrier, inc=1, device_id={"layer": me - 1}, device_id_type=pl.DeviceIdType.MESH)

    @pl.when(me < last)
    def _():
        pl.semaphore_signal(barrier, inc=1, device_id={"layer": me + 1}, device_id_type=pl.DeviceIdType.MESH)

    for offset in range(1, batch_axis):
        pl.semaphore_signal(
            barrier,
            inc=1,
            device_id={"batch": lax.rem(my_batch + offset, batch_axis)},
            device_id_type=pl.DeviceIdType.MESH,
        )
    others = batch_axis - 1 + jnp.where(me > 0, 1, 0) + jnp.where(me < last, 1, 0)
    pl.semaphore_wait(barrier, others)

    @pl.when(me < last)
    def _():
        for index in range(passes):
            guess_copy(index).start()

    @pl.when(me == 0)
    def _():
        pltpu.sync_copy(first_ref, guess_in)
        entry_in[...] = guess_in[...]

    for taps in (taps_0, taps_1, taps_2, taps_3):
        edge = jnp.zeros((width, 3 * channels), taps.dtype)
        taps[pl.ds(0, width), :] = edge
        taps[pl.ds((rows + 1) * width, width), :] = edge

    def put_taps(taps, index, count, block):
        flat = block.reshape(count * width, channels)
        column = lax.rem(lax.broadcasted_iota(jnp.int32, flat.shape, 0), width)
        before = jnp.where(column == 0, 0.0, pltpu.roll(flat, 1, 0))
        after = jnp.where(column == width - 1, 0.0, pltpu.roll(flat, count * width - 1, 0))
        at = pl.ds(pl.multiple_of((index * count + 1) * width, width), count * width)
        taps[at, pl.ds(0, channels)] = before.astype(taps.dtype)
        taps[at, pl.ds(channels, channels)] = flat.astype(taps.dtype)
        taps[at, pl.ds(2 * channels, channels)] = after.astype(taps.dtype)

    def mixed(taps, slot, index, count):
        total = None
        for down in range(3):
            at = pl.ds(pl.multiple_of((index * count + down) * width, width), count * width)
            part = jnp.dot(taps[at, :], weights_ref[slot, down], preferred_element_type=jnp.float32)
            total = part if total is None else total + part
        return jnp.maximum(total, 0.0).reshape(count, width, channels)

    def wave(count, arrive, steps):
        chunks = rows // count

        def body(turn, carry):
            @pl.when(turn < chunks)
            def _():
                arrive(turn)

            for behind, (taps, slot, emit) in enumerate(steps):
                index = turn - 1 - behind

                @pl.when(jnp.logical_and(index >= 0, index < chunks))
                def _(index=index, taps=taps, slot=slot, emit=emit):
                    emit(index, strip(index, count), mixed(taps, slot, index, count))

            return carry

        lax.fori_loop(0, chunks + len(steps), body, 0)

    load_weights.wait()

    def guess_arrives(index):
        @pl.when(me > 0)
        def _():
            guess_copy(index).wait_recv()

        put_taps(taps_0, index, PASS_ROWS, guess_in[strip(index, PASS_ROWS)])

    def relax_step(source, taps_next):
        def emit(index, at, active):
            block = source[at] + step_size * active
            work[at] = block
            put_taps(taps_next, index, PASS_ROWS, block)

        return emit

    def relax_last(index, at, active):
        relaxed_ref[at] = work[at] + step_size * active

        @pl.when(me < last)
        def _():
            entry_copy(index).start()

    wave(
        PASS_ROWS,
        guess_arrives,
        (
            (taps_0, 0, relax_step(guess_in, taps_1)),
            (taps_1, 1, relax_step(work, taps_2)),
            (taps_2, 2, relax_step(work, taps_3)),
            (taps_3, 3, relax_last),
        ),
    )

    def entry_arrives(index):
        @pl.when(me > 0)
        def _():
            entry_copy(index).wait_recv()

        put_taps(taps_0, index, PASS_ROWS, entry_in[strip(index, PASS_ROWS)])

    def sweep_first(index, at, active):
        block = entry_in[at]
        rhs_ref[at] = block + 4.0 * step_size * active
        block = block + step_size * active
        out_ref[0, at] = block
        put_taps(taps_1, index, PASS_ROWS, block)

    def sweep_middle(slot, count, taps_next):
        def emit(index, at, active):
            block = out_ref[slot - 1, at] + step_size * active
            out_ref[slot, at] = block
            if taps_next is not None:
                put_taps(taps_next, index, count, block)

        return emit

    def sweep_last(index, at, active):
        block = out_ref[2, at] + step_size * active
        out_ref[3, at] = block
        rhs_ref[at] = block - rhs_ref[at]

        @pl.when(jnp.logical_and(me == 1, me < last))
        def _():
            for piece in range(PASS_ROWS // CHAIN_ROWS):
                coarse_copy(index * (PASS_ROWS // CHAIN_ROWS) + piece).start()

        gap = (block - relaxed_ref[at]).reshape(-1, 8, channels)
        squares_ref[...] += jnp.sum(gap * gap, axis=0)

    squares_ref[...] = jnp.zeros_like(squares_ref)
    wave(
        PASS_ROWS,
        entry_arrives,
        (
            (taps_0, 0, sweep_first),
            (taps_1, 1, sweep_middle(1, PASS_ROWS, taps_2)),
            (taps_2, 2, sweep_middle(2, PASS_ROWS, taps_3)),
            (taps_3, 3, sweep_last),
        ),
    )
    partial_ref[my_batch] = squares_ref[...]
    for offset in range(1, batch_axis):
        norm_copy(offset).start()

    def coarse_arrives(index):
        coarse_copy(index).wait_recv()
        put_taps(taps_0, index, CHAIN_ROWS, coarse_in[strip(index, CHAIN_ROWS)])

    def chain_step(index, at, active):
        block = coarse_in[at]
        out_ref[3, at] = block + 4.0 * step_size * active + rhs_ref[at]

        @pl.when(me < last)
        def _():
            coarse_copy(index).start()

        block = block + step_size * active
        out_ref[0, at] = block
        put_taps(taps_1, index, CHAIN_ROWS, block)

    def run(taps, slot, count, emit):
        def body(index, carry):
            emit(index, strip(index, count), mixed(taps, slot, index, count))
            return carry

        return body

    chain_body = run(taps_0, 0, CHAIN_ROWS, chain_step)
    second_body = run(taps_1, 1, CHAIN_ROWS, sweep_middle(1, CHAIN_ROWS, taps_2))
    third_body = run(taps_2, 2, CHAIN_ROWS, sweep_middle(2, CHAIN_ROWS, None))

    @pl.when(me >= 2)
    def _():
        def body(turn, carry):
            coarse_arrives(turn)

            @pl.when(turn >= 1)
            def _():
                chain_body(turn - 1, 0)

            @pl.when(turn == pieces - 1)
            def _():
                chain_body(turn, 0)

            @pl.when(jnp.logical_and(me == last, turn >= 2))
            def _():
                second_body(turn - 2, 0)

            @pl.when(jnp.logical_and(me == last, turn >= 3))
            def _():
                third_body(turn - 3, 0)

            return carry

        lax.fori_loop(0, pieces, body, 0)

        @pl.when(me == last)
        def _():
            run(taps_1, 1, PASS_ROWS, sweep_middle(1, PASS_ROWS, taps_2))(passes - 1, 0)
            third_body(pieces - 3, 0)
            run(taps_2, 2, PASS_ROWS, sweep_middle(2, PASS_ROWS, None))(passes - 1, 0)

        @pl.when(me < last)
        def _():
            lax.fori_loop(0, passes, run(taps_1, 1, PASS_ROWS, sweep_middle(1, PASS_ROWS, taps_2)), 0)
            lax.fori_loop(0, passes, run(taps_2, 2, PASS_ROWS, sweep_middle(2, PASS_ROWS, None)), 0)

    for offset in range(1, batch_axis):
        norm_copy(offset).wait()
    gathered = partial_ref[0]
    for index in range(1, batch_axis):
        gathered = gathered + partial_ref[index]
    entries = rows * width * channels * batch_axis
    norm_ref[...] = jnp.broadcast_to(jnp.sqrt(jnp.sum(gathered, keepdims=True) / entries + 1e-06), norm_ref.shape)

    @pl.when(me < last)
    def _():
        for index in range(passes):
            guess_copy(index).wait_send()
            entry_copy(index).wait_send()

    @pl.when(jnp.logical_and(me >= 1, me < last))
    def _():
        for index in range(pieces):
            coarse_copy(index).wait_send()


def per_device_streamed(first_state, guess_points, weights):
    layers_axis = lax.axis_size("layer")
    batch_axis = lax.axis_size("batch")
    _, rows, width, channels = first_state.shape
    state = (rows, width, channels)
    taps = ((rows + 2) * width, 3 * channels)
    passes, pieces = rows // PASS_ROWS, rows // CHAIN_ROWS
    in_vmem = pl.BlockSpec(memory_space=pltpu.VMEM)
    states, norms = pl.pallas_call(
        functools.partial(cycle_kernel, layers_axis, batch_axis),
        out_shape=(
            pltpu.VMEM((BLOCK,) + state, jnp.float32),
            jax.ShapeDtypeStruct((8, 128), jnp.float32),
        ),
        in_specs=[pl.BlockSpec(memory_space=pltpu.HBM)] * 3,
        out_specs=(in_vmem, in_vmem),
        scratch_shapes=[pltpu.VMEM(state, jnp.float32)] * 6
        + [pltpu.VMEM(taps, jnp.bfloat16)] * 4
        + [pltpu.VMEM((8, channels), jnp.float32)]
        + [pltpu.VMEM((BLOCK, 3, 3 * channels, channels), jnp.bfloat16), pltpu.SemaphoreType.DMA]
        + [pltpu.VMEM((batch_axis, 8, channels), jnp.float32)]
        + [pltpu.SemaphoreType.DMA((passes,))] * 4
        + [pltpu.SemaphoreType.DMA((pieces,))] * 2
        + [pltpu.SemaphoreType.DMA((batch_axis,))] * 2,
        compiler_params=pltpu.CompilerParams(
            collective_id=0, has_side_effects=True, vmem_limit_bytes=40 * 1024 * 1024
        ),
    )(*(pltpu.with_memory_space_constraint(x, pltpu.HBM) for x in (first_state[0], guess_points[0, 0], weights.reshape(BLOCK, 3, 3 * channels, channels))))
    return (states[:, None], norms[0, :1])


def solution(mesh):
    placed = (
        P("batch", None, None, None),
        P("layer", "batch", None, None, None),
        P("layer", None, None, None, None),
    )
    return jax.shard_map(
        per_device if mesh.shape["layer"] // BLOCK > 2 else per_device_streamed,
        mesh=mesh,
        in_specs=placed,
        out_specs=(P("layer", "batch", None, None, None), P("layer")),
        check_vma=False,
    )
```
